256 devices in a mesh: dp: 8 (over y, x_lo), mp: 32 (over x_hi, z, core).
Axes of the slice: x: 4 (x_hi: 2, x_lo: 2; x = x_hi * 2 + x_lo), y: 4, z: 8, core: 2. Of those that a mesh axis runs over, the one named last changes fastest.
Arguments:
- activations: bfloat16 [512, 28672], P('dp', 'mp'), may hold values from -6 to 6
- out_grads: bfloat16 [512, 8192], P('mp', 'dp'), may hold values from -6 to 6
- act_basis: bfloat16 [28672, 28672], P('dp', 'mp'), may hold values from -0.03125 to 0.03125
- grad_basis: bfloat16 [8192, 8192], P('mp', 'dp'), may hold values from -0.0625 to 0.0625
Outputs:
- correction: float32 [8192, 28672], P('mp', 'dp')
The draws below stay inside these ranges and needn't reach their ends.
All inputs are finite; a program needn't handle non-finite values.
Results may differ from the reference program's by a relative error of at most 0.0041.
Values may be sent and summed in bfloat16 or wider, within the bound.
No kernel may reach another device: no remote copies, remote signals or barrier semaphores. Data moves between devices by JAX's collectives and lax.ppermute only.
A program may use at most 64 MiB of HBM per device.

```python
import jax
import jax.numpy as jnp
from jax import lax

D_IN = 28672
D_OUT = 8192
SEQ_LEN = 256
SEQS = 2
TOKENS = 512


def block_levels(rng, shape, pieces, smallest, largest):
    loudness, own = 1.0, jax.random.fold_in(rng, 6)
    for position, parts in pieces:
        steps = jnp.exp(jax.random.uniform(jax.random.fold_in(own, position), (parts,), jnp.float32, smallest / len(pieces), largest / len(pieces)))
        loudness = loudness * jnp.repeat(steps, shape[position] // parts).reshape([-1 if axis == position else 1 for axis in range(len(shape))])
    return loudness


def bell_draw(key, dims, spread, limit, pieces=(), kind=jnp.bfloat16):
    values = spread * jax.random.normal(key, dims, jnp.float32)
    if pieces:
        values = values * block_levels(key, dims, pieces, -0.22, 0.18)
    return jnp.clip(values, -limit, limit).astype(kind)


def setup_inputs(seed: int = 0) -> dict:
    splits = jax.random.split(jax.random.key(seed), 5)
    return {
        "activations": bell_draw(splits[0], (TOKENS, D_IN), 1.0, 6.0, ((0, 8), (1, 32))),
        "out_grads": bell_draw(splits[1], (TOKENS, D_OUT), 1.0, 6.0, ((0, 32), (1, 8))),
        "act_basis": bell_draw(splits[2], (D_IN, D_IN), D_IN ** -0.5, 0.03125, ((0, 8), (1, 32))),
        "grad_basis": bell_draw(splits[3], (D_OUT, D_OUT), D_OUT ** -0.5, 0.0625, ((0, 32), (1, 8))),
    }


def rotate(rows, basis):
    return lax.dot_general(rows, basis, (((1,), (1,)), ((), ())), preferred_element_type=jnp.float32)


def reference(activations, out_grads, act_basis, grad_basis):
    act_rotated = rotate(activations, act_basis).astype(jnp.bfloat16)
    grad_rotated = rotate(out_grads, grad_basis).astype(jnp.bfloat16)
    act_seqs = act_rotated.reshape(SEQS, SEQ_LEN, D_IN)
    grad_seqs = grad_rotated.reshape(SEQS, SEQ_LEN, D_OUT)

    def accumulate(total, pair):
        grad_block, act_block = pair
        seq_grad = lax.dot_general(grad_block, act_block, (((0,), (0,)), ((), ())), preferred_element_type=jnp.float32)
        return total + seq_grad * seq_grad, None

    total, unused = lax.scan(accumulate, jnp.zeros((D_OUT, D_IN), jnp.float32), (grad_seqs, act_seqs))
    return total / jnp.float32(SEQS * SEQ_LEN)
```

```python
import functools

import jax
import jax.numpy as jnp
from jax import lax
from jax.experimental import pallas as pl
from jax.experimental.pallas import tpu as pltpu
from jax.sharding import PartitionSpec as P

SEQ_LEN = 256
BF, F32 = jnp.bfloat16, jnp.float32
STREAMS = 2
TILE = 256


def mp_at(h, z, c):
    return ((h % 2) * 8 + z % 8) * 2 + c % 2


def dp_at(y, l):
    return (y % 4) * 2 + l % 2


def mp_perm(f):
    return [(mp_at(h, z, c), mp_at(*f(h, z, c))) for h in range(2) for z in range(8) for c in range(2)]


def dp_perm(f):
    return [(dp_at(y, l), dp_at(*f(y, l))) for y in range(4) for l in range(2)]


CORE = mp_perm(lambda h, z, c: (h, z, c + 1))
XHI = mp_perm(lambda h, z, c: (h + 1, z, c))
AHEAD = mp_perm(lambda h, z, c: (h, z + 1 - 2 * c, c))
XLO = dp_perm(lambda y, l: (y, l + 1))
Y1 = dp_perm(lambda y, l: (y ^ 1, l))
Y2 = dp_perm(lambda y, l: (y ^ 2, l))


def swap(x):
    return lax.ppermute(x, "mp", CORE)


def ahead(x):
    return lax.ppermute(x, "mp", AHEAD)


def across(x):
    return lax.ppermute(x, "mp", XHI)


def after(x, *others):
    return lax.optimization_barrier((x,) + others)[0]


def dot_t(a, b):
    return lax.dot_general(a, b, (((1,), (1,)), ((), ())), preferred_element_type=F32)


def token_row(place, step, other):
    z, c, y, l = place
    block = lax.rem(z + (1 - 2 * c) * step + 16, 8)
    source = lax.rem(y + 4 - block // 2, 4) * 2 + lax.rem(l + block, 2)
    half = 1 - c if other else c
    return pl.multiple_of(source * 64 + half * 32, 32)


def finish_kernel(width, first, aliased, place_ref, g_ref, *refs):
    blocks, refs = refs[:10], refs[10 + aliased :]
    out_ref, act, tile, out_sem = refs
    place = [place_ref[i] for i in range(4)]
    own, twin, a1, a2, a3, a4, b1, b2, b3, b4 = blocks

    def put(ref, row, step, other):
        act[pl.ds(token_row(place, step, other), 32)] = ref[row : row + 32]

    put(own, 0, 0, False)
    put(twin, 0, 0, True)
    for k, a, b in ((1, a1, b1), (2, a2, b2), (3, a3, b3)):
        put(a, 0, -k, False)
        put(a, 32, -k, True)
        put(b, 0, k, True)
        put(b, 32, k, False)
    put(a4, 0, 4, False)
    put(b4, 0, 4, True)
    writes = []
    for t in range(width // TILE):
        total = None
        for s in range(2):
            rows = slice(s * SEQ_LEN, (s + 1) * SEQ_LEN)
            part = jnp.dot(g_ref[:, rows], act[rows, t * TILE : (t + 1) * TILE], preferred_element_type=F32)
            total = part * part if total is None else total + part * part
        tile[t] = total * F32(1 / 512)
        write = pltpu.make_async_copy(tile.at[t], out_ref.at[:, pl.ds(first + t * TILE, TILE)], out_sem.at[t])
        write.start()
        writes.append(write)
    for write in writes:
        write.wait()


def finish(place, g, blocks, width, first, whole, rest):
    aliased = rest is not None
    vmem, hbm = pl.BlockSpec(memory_space=pltpu.VMEM), pl.BlockSpec(memory_space=pl.ANY)
    tiles = width // TILE
    return pl.pallas_call(
        functools.partial(finish_kernel, width, first, int(aliased)),
        out_shape=jax.ShapeDtypeStruct((256, whole), F32),
        in_specs=[pl.BlockSpec(memory_space=pltpu.SMEM)] + [vmem] * (1 + len(blocks)) + [hbm] * aliased,
        out_specs=hbm,
        scratch_shapes=[
            pltpu.VMEM((512, width), BF),
            pltpu.VMEM((tiles, 256, TILE), F32),
            pltpu.SemaphoreType.DMA((tiles,)),
        ],
        input_output_aliases={2 + len(blocks): 0} if aliased else {},
        compiler_params=pltpu.CompilerParams(vmem_limit_bytes=12 * 1024 * 1024),
        cost_estimate=pl.CostEstimate(flops=2 * 512 * 256 * width, bytes_accessed=width * (1024 + 1024), transcendentals=0),
        name="finish",
    )(place, g, *blocks, *([rest] if aliased else []))


N0 = [(0, o, d) for o in (0, 1) for d in (0, 1)]
NEAR = [(-k, o, d) for k in (1, 2, 3) for o in (0, 1) for d in (0, 1)] + [(4, 0, d) for d in (0, 1)]
FAR = [(k, 1 - o, d) for k in (1, 2, 3) for o in (0, 1) for d in (0, 1)] + [(4, 1, d) for d in (0, 1)]


def rotate_grads_kernel(place_ref, n0_ref, near_ref, far_ref, basis_ref, out_ref, rows):
    z, c, h = place_ref[0], place_ref[1], place_ref[4]
    for ref, pieces in ((n0_ref, N0), (near_ref, NEAR), (far_ref, FAR)):
        for piece, (step, other, pair) in enumerate(pieces):
            z2 = lax.rem(z + (1 - 2 * c) * step + 16, 8)
            h2 = 1 - h if pair else h
            c2 = 1 - c if other else c
            row = pl.multiple_of(((h2 * 8 + z2) * 2 + c2) * 16, 16)
            rows[pl.ds(row, 16)] = ref[piece * 16 : (piece + 1) * 16]
    out_ref[...] = lax.dot_general(
        basis_ref[...], rows[...], (((1,), (1,)), ((), ())), preferred_element_type=F32
    )


def rotate_grads(place, n0, near, far, basis):
    vmem = pl.BlockSpec(memory_space=pltpu.VMEM)
    return pl.pallas_call(
        rotate_grads_kernel,
        out_shape=jax.ShapeDtypeStruct((256, 512), F32),
        in_specs=[pl.BlockSpec(memory_space=pltpu.SMEM)] + [vmem] * 4,
        out_specs=vmem,
        scratch_shapes=[pltpu.VMEM((512, 1024), BF)],
        compiler_params=pltpu.CompilerParams(vmem_limit_bytes=8 * 1024 * 1024),
        cost_estimate=pl.CostEstimate(flops=2 * 512 * 256 * 1024, bytes_accessed=2 << 20, transcendentals=0),
        name="rotate_grads",
    )(place, n0, near, far, basis)


def shards(activations, out_grads, act_basis, grad_basis):
    mp, dp = lax.axis_index("mp"), lax.axis_index("dp")
    c, z, h = mp % 2, (mp // 2) % 8, mp // 16
    y, l = dp // 2, dp % 2
    sign = 1 - 2 * c
    place = jnp.stack([z, c, y, l, h]).astype(jnp.int32)

    pair = jnp.concatenate([out_grads, swap(out_grads)])
    basis_away = swap(after(act_basis, pair))

    def shift(x, b):
        return lax.ppermute(x, "dp", dp_perm(lambda y, l: (y + b // 2, l + b % 2)))

    blocks = [activations] + [None] * 7
    for b in (4, 2, 6, 1):
        blocks[b] = shift(activations, b)
    far = across(pair)
    blocks[3] = shift(blocks[1], 2)
    blocks[7] = shift(blocks[1], 6)
    blocks[5] = shift(blocks[4], 1)
    n0 = jnp.concatenate([pair[:16], far[:16], pair[16:], far[16:]])
    n1 = ahead(n0)
    halves = jnp.stack(blocks).reshape(16, 32, -1)

    def half(step, other):
        return lax.dynamic_index_in_dim(halves, (z + sign * step) % 8 * 2 + (1 - c if other else c), 0, keepdims=False)

    mine = [half(s, o) for s in (1, 2, 3) for o in (False, True)] + [half(4, False), half(0, False)]
    theirs = [half(-s, o) for s in (1, 2, 3) for o in (True, False)] + [half(4, True), half(0, True)]
    x_here = jnp.concatenate(mine)
    x_away = swap(jnp.concatenate(theirs))
    n2 = ahead(after(n1, x_here))

    whole = act_basis.shape[0]
    width = whole // STREAMS
    streams = range(STREAMS)
    cols = [slice(s * width, (s + 1) * width) for s in streams]
    p = [dot_t(x_here, act_basis[k]) + dot_t(x_away, basis_away[k]) for k in cols]
    r = [ahead(p[s][192:224].astype(BF)) for s in streams]
    n3 = ahead(after(n2, p[0]))
    n4 = ahead(after(n3[:32], r[0]))
    r = [ahead(jnp.concatenate([p[s][128:160] + r[s].astype(F32), p[s][160:192]]).astype(BF)) for s in streams]
    near = after(jnp.concatenate([n1, n2, n3, n4]), r[0])
    g = rotate_grads(place, n0, near, swap(near), grad_basis)
    g_away = lax.ppermute(g, "dp", Y1)
    r = [ahead((p[s][64:128] + r[s].astype(F32)).astype(BF)) for s in streams]
    r = [ahead((p[s][0:64] + r[s].astype(F32)).astype(BF)) for s in streams]
    r = [p[s][224:256] + r[s][:32].astype(F32) + swap(r[s][32:]).astype(F32) for s in streams]
    g = g + after(g_away, r[0])
    g_away = lax.ppermute(g, "dp", Y2)
    own = [(r[s] + across(r[s].astype(BF)).astype(F32)).astype(BF) for s in streams]

    twin = [swap(own[s]) for s in streams]
    a1 = [ahead(jnp.concatenate([own[s], twin[s]])) for s in streams]
    b1 = [swap(a) for a in a1]
    a2 = [ahead(a) for a in a1]
    g = g + after(g_away, a1[1])
    g_away = lax.ppermute(g, "dp", XLO)
    b2 = [swap(a) for a in a2]
    a3 = [ahead(a) for a in a2]
    b3 = [swap(a) for a in a3]
    a4 = [ahead(a[:32]) for a in a3]
    b4 = [swap(a) for a in a4]
    g = (g + after(g_away, a3[1])).astype(BF)
    out = None
    for s in streams:
        parts = [x[s] for x in (own, twin, a1, a2, a3, a4, b1, b2, b3, b4)]
        out = finish(place, g, parts, width, s * width, whole, out)
    return out


def solution(mesh):
    return jax.shard_map(
        shards,
        mesh=mesh,
        in_specs=(P("dp", "mp"), P("mp", "dp"), P("dp", "mp"), P("mp", "dp")),
        out_specs=P("mp", "dp"),
        check_vma=False,
    )
```

```python
import functools

import jax
import jax.numpy as jnp
from jax import lax
from jax.experimental import pallas as pl
from jax.experimental.pallas import tpu as pltpu
from jax.sharding import PartitionSpec as P

SEQ_LEN = 256
BF, F32 = jnp.bfloat16, jnp.float32
TILE = 256
STREAMS = 2


def mp_at(h, z, c):
    return ((h % 2) * 8 + z % 8) * 2 + c % 2


def dp_at(y, l):
    return (y % 4) * 2 + l % 2


def mp_perm(f):
    return [(mp_at(h, z, c), mp_at(*f(h, z, c))) for h in range(2) for z in range(8) for c in range(2)]


def dp_perm(f):
    return [(dp_at(y, l), dp_at(*f(y, l))) for y in range(4) for l in range(2)]


CORE = mp_perm(lambda h, z, c: (h, z, c + 1))
XHI = mp_perm(lambda h, z, c: (h + 1, z, c))
AHEAD = mp_perm(lambda h, z, c: (h, z + 1 - 2 * c, c))
AHEAD2 = mp_perm(lambda h, z, c: (h, z + 2 - 4 * c, c))
XLO = dp_perm(lambda y, l: (y, l + 1))
Y1 = dp_perm(lambda y, l: (y ^ 1, l))
Y2 = dp_perm(lambda y, l: (y ^ 2, l))


def swap(x, name="swap"):
    with jax.named_scope(name):
        return lax.ppermute(x, "mp", CORE)


def ahead(x, name="ahead"):
    with jax.named_scope(name):
        return lax.ppermute(x, "mp", AHEAD)


def ahead2(x, name="ahead2"):
    with jax.named_scope(name):
        return lax.ppermute(x, "mp", AHEAD2)


def across(x, name="across"):
    with jax.named_scope(name):
        return lax.ppermute(x, "mp", XHI)


def after(x, *others):
    return lax.optimization_barrier((x,) + others)[0]


def dot_t(a, b):
    return lax.dot_general(a, b, (((1,), (1,)), ((), ())), preferred_element_type=F32)


def cat(*parts):
    return jnp.concatenate(parts)


def block(step):
    return [(step, 0), (step, 1)]


def mirrored(halves):
    return [(-step if abs(step) < 4 else step, 1 - other) for step, other in halves]


LAYOUT = [[(0, 0)], [(0, 1)], block(-1), block(-2), block(-3), [(4, 0)]]
LAYOUT = LAYOUT + [mirrored(block(-1) + block(-2)), mirrored(block(-3) + [(4, 0)])]


def finish_kernel(width, first, aliased, place_ref, g_ref, *refs):
    blocks, refs = refs[: len(LAYOUT)], refs[len(LAYOUT) + aliased :]
    out_ref, act, tile, out_sem = refs
    z, c, y, l = [place_ref[i] for i in range(4)]
    for ref, halves in zip(blocks, LAYOUT):
        for i, (step, other) in enumerate(halves):
            b = lax.rem(z + (1 - 2 * c) * step + 16, 8)
            source = lax.rem(y + 4 - b // 2, 4) * 2 + lax.rem(l + b, 2)
            row = pl.multiple_of(source * 64 + (1 - c if other else c) * 32, 32)
            act[pl.ds(row, 32)] = ref[i * 32 : (i + 1) * 32]
    writes = []
    for t in range(width // TILE):
        total = None
        for s in range(2):
            rows = slice(s * SEQ_LEN, (s + 1) * SEQ_LEN)
            part = jnp.dot(g_ref[:, rows], act[rows, t * TILE : (t + 1) * TILE], preferred_element_type=F32)
            total = part * part if total is None else total + part * part
        tile[t] = total * F32(1 / 512)
        write = pltpu.make_async_copy(tile.at[t], out_ref.at[:, pl.ds(first + t * TILE, TILE)], out_sem.at[t])
        write.start()
        writes.append(write)
    for write in writes:
        write.wait()


def finish(place, g, blocks, width, first, whole, rest):
    aliased = rest is not None
    vmem, hbm = pl.BlockSpec(memory_space=pltpu.VMEM), pl.BlockSpec(memory_space=pl.ANY)
    tiles = width // TILE
    return pl.pallas_call(
        functools.partial(finish_kernel, width, first, int(aliased)),
        out_shape=jax.ShapeDtypeStruct((256, whole), F32),
        in_specs=[pl.BlockSpec(memory_space=pltpu.SMEM)] + [vmem] * (1 + len(blocks)) + [hbm] * aliased,
        out_specs=hbm,
        scratch_shapes=[
            pltpu.VMEM((512, width), BF),
            pltpu.VMEM((tiles, 256, TILE), F32),
            pltpu.SemaphoreType.DMA((tiles,)),
        ],
        input_output_aliases={2 + len(blocks): 0} if aliased else {},
        compiler_params=pltpu.CompilerParams(vmem_limit_bytes=12 * 1024 * 1024),
        cost_estimate=pl.CostEstimate(flops=2 * 512 * 256 * width, bytes_accessed=width * (1024 + 1024), transcendentals=0),
        name="finish",
    )(place, g, *blocks, *([rest] if aliased else []))


def quarters(halves):
    return [(step, other, pair) for step, other in halves for pair in (0, 1)]


N0 = quarters(block(0))
NEAR = quarters(block(-2) + block(-1) + block(-3) + [(4, 0)])
FAR = quarters(mirrored(block(-2) + block(-1) + block(-3) + [(4, 0)]))


def rotate_grads_kernel(place_ref, n0_ref, near_ref, far_ref, basis_ref, out_ref, rows):
    z, c, h = place_ref[0], place_ref[1], place_ref[4]
    for ref, pieces in ((n0_ref, N0), (near_ref, NEAR), (far_ref, FAR)):
        for piece, (step, other, pair) in enumerate(pieces):
            z2 = lax.rem(z + (1 - 2 * c) * step + 16, 8)
            h2 = 1 - h if pair else h
            c2 = 1 - c if other else c
            row = pl.multiple_of(((h2 * 8 + z2) * 2 + c2) * 16, 16)
            rows[pl.ds(row, 16)] = ref[piece * 16 : (piece + 1) * 16]
    out_ref[...] = lax.dot_general(
        basis_ref[...], rows[...], (((1,), (1,)), ((), ())), preferred_element_type=F32
    )


def rotate_grads(place, n0, near, far, basis):
    vmem = pl.BlockSpec(memory_space=pltpu.VMEM)
    return pl.pallas_call(
        rotate_grads_kernel,
        out_shape=jax.ShapeDtypeStruct((256, 512), F32),
        in_specs=[pl.BlockSpec(memory_space=pltpu.SMEM)] + [vmem] * 4,
        out_specs=vmem,
        scratch_shapes=[pltpu.VMEM((512, 1024), BF)],
        compiler_params=pltpu.CompilerParams(vmem_limit_bytes=8 * 1024 * 1024),
        cost_estimate=pl.CostEstimate(flops=2 * 512 * 256 * 1024, bytes_accessed=2 << 20, transcendentals=0),
        name="rotate_grads",
    )(place, n0, near, far, basis)


def arrange_kernel(place_ref, *refs):
    blocks, (mine_ref, theirs_ref, rows) = refs[:8], refs[8:]
    z, c = place_ref[0], place_ref[1]
    for b, ref in enumerate(blocks):
        k = lax.rem((b - z) * (1 - 2 * c) + 16, 8)
        for core in range(2):
            other = jnp.where(c == core, 0, 1)
            centre = jnp.where(k == 0, 224, 192) + other * 256
            ring = jnp.where(k < 4, (k - 1) * 64 + other * 32, 256 + (7 - k) * 64 + (1 - other) * 32)
            row = pl.multiple_of(jnp.where((k == 0) | (k == 4), centre, ring), 32)
            rows[pl.ds(row, 32)] = ref[core * 32 : core * 32 + 32]
    mine_ref[...] = rows[:256]
    theirs_ref[...] = rows[256:]


def arrange(place, blocks):
    vmem = pl.BlockSpec(memory_space=pltpu.VMEM)
    depth = blocks[0].shape[1]
    rows = jax.ShapeDtypeStruct((256, depth), BF)
    return pl.pallas_call(
        arrange_kernel,
        out_shape=(rows, rows),
        in_specs=[pl.BlockSpec(memory_space=pltpu.SMEM)] + [vmem] * 8,
        out_specs=(vmem, vmem),
        scratch_shapes=[pltpu.VMEM((512, depth), BF)],
        compiler_params=pltpu.CompilerParams(vmem_limit_bytes=8 * 1024 * 1024),
        cost_estimate=pl.CostEstimate(flops=0, bytes_accessed=4 * 512 * depth, transcendentals=0),
        name="arrange",
    )(place, *blocks)


def rotate_here_kernel(rows_ref, basis_ref, out_ref):
    for t in range(0, out_ref.shape[1], TILE):
        out_ref[:, t : t + TILE] = dot_t(rows_ref[...], basis_ref[t : t + TILE])


def rotate_here(rows, basis):
    vmem = pl.BlockSpec(memory_space=pltpu.VMEM)
    whole, depth = basis.shape
    return pl.pallas_call(
        rotate_here_kernel,
        out_shape=jax.ShapeDtypeStruct((256, whole), F32),
        in_specs=[vmem] * 2,
        out_specs=vmem,
        compiler_params=pltpu.CompilerParams(vmem_limit_bytes=16 * 1024 * 1024),
        cost_estimate=pl.CostEstimate(flops=512 * depth * whole, bytes_accessed=2 * depth * whole, transcendentals=0),
        name="rotate_here",
    )(rows, basis)


def rotate_away_kernel(part_ref, rows_ref, basis_ref, *out_refs):
    width = out_refs[0].shape[1]
    for t in range(0, part_ref.shape[1], TILE):
        total = part_ref[:, t : t + TILE] + dot_t(rows_ref[...], basis_ref[t : t + TILE])
        out_refs[t // width][:, t % width : t % width + TILE] = total


def rotate_away(part, rows, basis):
    vmem = pl.BlockSpec(memory_space=pltpu.VMEM)
    whole, depth = basis.shape
    return pl.pallas_call(
        rotate_away_kernel,
        out_shape=[jax.ShapeDtypeStruct((256, whole // STREAMS), F32)] * STREAMS,
        in_specs=[vmem] * 3,
        out_specs=[vmem] * STREAMS,
        compiler_params=pltpu.CompilerParams(vmem_limit_bytes=20 * 1024 * 1024),
        cost_estimate=pl.CostEstimate(flops=512 * depth * whole, bytes_accessed=2 * depth * whole, transcendentals=0),
        name="rotate_away",
    )(part, rows, basis)


def shards(activations, out_grads, act_basis, grad_basis):
    mp, dp = lax.axis_index("mp"), lax.axis_index("dp")
    c, z, h = mp % 2, (mp // 2) % 8, mp // 16
    y, l = dp // 2, dp % 2
    place = jnp.stack([z, c, y, l, h]).astype(jnp.int32)

    pair = cat(out_grads, swap(out_grads, "out_grads_pair"))

    def shift(x, b):
        with jax.named_scope(f"activations_{b}"):
            return lax.ppermute(x, "dp", dp_perm(lambda y, l: (y + b // 2, l + b % 2)))

    blocks = [activations] + [None] * 7
    for b in (4, 2, 6, 1):
        blocks[b] = shift(activations, b)
    basis_away = swap(after(act_basis, pair), "basis_away")
    far = across(pair, "far")
    blocks[3] = shift(blocks[1], 2)
    blocks[7] = shift(blocks[1], 6)
    blocks[5] = shift(blocks[4], 1)
    n0 = cat(pair[:16], far[:16], pair[16:], far[16:])
    n2 = ahead2(n0, "n2")
    x_here, theirs = arrange(place, blocks)
    x_away = swap(theirs, "x_away")
    part = rotate_here(x_here, act_basis)
    n02 = cat(n0, n2)
    n13 = ahead(n02, "n13")
    n4 = ahead2(n2[:32], "n4")

    whole = act_basis.shape[0]
    width = whole // STREAMS
    streams = range(STREAMS)
    p = rotate_away(part, x_away, basis_away)

    r = [ahead(p[s][192:224].astype(BF), f"step1_{s}") for s in streams]
    near = after(cat(n2, n13, n4), p[0])
    g = rotate_grads(place, n0, near, swap(near, "near_away"), grad_basis)
    g_away = lax.ppermute(g, "dp", Y1)
    r = [cat(p[s][128:160] + r[s].astype(F32), p[s][160:192]).astype(BF) for s in streams]
    r = [ahead(r[s], f"step2_{s}") for s in streams]
    r[0] = after(r[0], g)
    r = [ahead((p[s][64:128] + r[s].astype(F32)).astype(BF), f"step3_{s}") for s in streams]
    r = [ahead((p[s][0:64] + r[s].astype(F32)).astype(BF), f"step4_{s}") for s in streams]
    g = g + g_away
    g_away = lax.ppermute(g, "dp", Y2)
    r[1] = after(r[1], g)
    r = [p[s][224:256] + r[s][:32].astype(F32) + swap(r[s][32:], f"other_{s}").astype(F32) for s in streams]
    own = [(r[s] + across(r[s].astype(BF), f"across_{s}").astype(F32)).astype(BF) for s in streams]

    twin = [swap(own[s], f"twin_{s}") for s in streams]
    a1 = [ahead(cat(own[s], twin[s]), f"a1_{s}") for s in streams]
    g = g + g_away
    g_away = lax.ppermute(g, "dp", XLO)
    a1[0] = after(a1[0], g)
    a2 = [ahead(a1[s], f"a2_{s}") for s in streams]
    b12 = [swap(cat(a1[s], a2[s]), f"b12_{s}") for s in streams]
    a3 = [ahead(a2[s], f"a3_{s}") for s in streams]
    g = (g + g_away).astype(BF)
    a4 = [ahead(after(a3[s][:32], g), f"a4_{s}") for s in streams]
    b34 = [swap(cat(a3[s], a4[s]), f"b34_{s}") for s in streams]
    out = None
    for s in streams:
        parts = [x[s] for x in (own, twin, a1, a2, a3, a4, b12, b34)]
        out = finish(place, g, parts, width, s * width, whole, out)
    return out


def solution(mesh):
    return jax.shard_map(
        shards,
        mesh=mesh,
        in_specs=(P("dp", "mp"), P("mp", "dp"), P("dp", "mp"), P("mp", "dp")),
        out_specs=P("mp", "dp"),
        check_vma=False,
    )
```

```python
import functools

import jax
import jax.numpy as jnp
from jax import lax
from jax.experimental import pallas as pl
from jax.experimental.pallas import tpu as pltpu
from jax.sharding import PartitionSpec as P

SEQ_LEN = 256
BF, F32 = jnp.bfloat16, jnp.float32
TILE = 256
STREAMS = 2


def mp_at(h, z, c):
    return ((h % 2) * 8 + z % 8) * 2 + c % 2


def dp_at(y, l):
    return (y % 4) * 2 + l % 2


def mp_perm(f):
    return [(mp_at(h, z, c), mp_at(*f(h, z, c))) for h in range(2) for z in range(8) for c in range(2)]


def dp_perm(f):
    return [(dp_at(y, l), dp_at(*f(y, l))) for y in range(4) for l in range(2)]


CORE = mp_perm(lambda h, z, c: (h, z, c + 1))
XHI = mp_perm(lambda h, z, c: (h + 1, z, c))
AHEAD = mp_perm(lambda h, z, c: (h, z + 1 - 2 * c, c))
AHEAD2 = mp_perm(lambda h, z, c: (h, z + 2 - 4 * c, c))
XLO = dp_perm(lambda y, l: (y, l + 1))
Y1 = dp_perm(lambda y, l: (y ^ 1, l))
Y2 = dp_perm(lambda y, l: (y ^ 2, l))


def swap(x, name="swap"):
    with jax.named_scope(name):
        return lax.ppermute(x, "mp", CORE)


def ahead(x, name="ahead"):
    with jax.named_scope(name):
        return lax.ppermute(x, "mp", AHEAD)


def ahead2(x, name="ahead2"):
    with jax.named_scope(name):
        return lax.ppermute(x, "mp", AHEAD2)


def across(x, name="across"):
    with jax.named_scope(name):
        return lax.ppermute(x, "mp", XHI)


def after(x, *others):
    return lax.optimization_barrier((x,) + others)[0]


def dot_t(a, b):
    return lax.dot_general(a, b, (((1,), (1,)), ((), ())), preferred_element_type=F32)


def cat(*parts):
    return jnp.concatenate(parts)


def block(step):
    return [(step, 0), (step, 1)]


def mirrored(halves):
    return [(-step if abs(step) < 4 else step, 1 - other) for step, other in halves]


LAYOUT = [[(0, 0)], [(0, 1)], block(-1), block(-2), block(-3), [(4, 0)]]
LAYOUT = LAYOUT + [mirrored(block(-1) + block(-2)), mirrored(block(-3) + [(4, 0)])]


def finish_kernel(width, first, aliased, place_ref, g_ref, *refs):
    blocks, refs = refs[: len(LAYOUT)], refs[len(LAYOUT) + aliased :]
    out_ref, act, tile, out_sem = refs
    z, c, y, l = [place_ref[i] for i in range(4)]
    for ref, halves in zip(blocks, LAYOUT):
        for i, (step, other) in enumerate(halves):
            b = lax.rem(z + (1 - 2 * c) * step + 16, 8)
            source = lax.rem(y + 4 - b // 2, 4) * 2 + lax.rem(l + b, 2)
            row = pl.multiple_of(source * 64 + (1 - c if other else c) * 32, 32)
            act[pl.ds(row, 32)] = ref[i * 32 : (i + 1) * 32]
    writes = []
    for t in range(width // TILE):
        total = None
        for s in range(2):
            rows = slice(s * SEQ_LEN, (s + 1) * SEQ_LEN)
            part = jnp.dot(g_ref[:, rows], act[rows, t * TILE : (t + 1) * TILE], preferred_element_type=F32)
            total = part * part if total is None else total + part * part
        tile[t] = total * F32(1 / 512)
        write = pltpu.make_async_copy(tile.at[t], out_ref.at[:, pl.ds(first + t * TILE, TILE)], out_sem.at[t])
        write.start()
        writes.append(write)
    for write in writes:
        write.wait()


def finish(place, g, blocks, width, first, whole, rest):
    aliased = rest is not None
    vmem, hbm = pl.BlockSpec(memory_space=pltpu.VMEM), pl.BlockSpec(memory_space=pl.ANY)
    tiles = width // TILE
    return pl.pallas_call(
        functools.partial(finish_kernel, width, first, int(aliased)),
        out_shape=jax.ShapeDtypeStruct((256, whole), F32),
        in_specs=[pl.BlockSpec(memory_space=pltpu.SMEM)] + [vmem] * (1 + len(blocks)) + [hbm] * aliased,
        out_specs=hbm,
        scratch_shapes=[
            pltpu.VMEM((512, width), BF),
            pltpu.VMEM((tiles, 256, TILE), F32),
            pltpu.SemaphoreType.DMA((tiles,)),
        ],
        input_output_aliases={2 + len(blocks): 0} if aliased else {},
        compiler_params=pltpu.CompilerParams(vmem_limit_bytes=12 * 1024 * 1024),
        cost_estimate=pl.CostEstimate(flops=2 * 512 * 256 * width, bytes_accessed=width * (1024 + 1024), transcendentals=0),
        name="finish",
    )(place, g, *blocks, *([rest] if aliased else []))


def quarters(halves):
    return [(step, other, pair) for step, other in halves for pair in (0, 1)]


N0 = quarters(block(0))
NEAR = quarters(block(-2) + block(-1) + block(-3) + [(4, 0)])
FAR = quarters(mirrored(block(-2) + block(-1) + block(-3) + [(4, 0)]))


def rotate_grads_kernel(place_ref, n0_ref, near_ref, far_ref, basis_ref, out_ref, rows):
    z, c, h = place_ref[0], place_ref[1], place_ref[4]
    for ref, pieces in ((n0_ref, N0), (near_ref, NEAR), (far_ref, FAR)):
        for piece, (step, other, pair) in enumerate(pieces):
            z2 = lax.rem(z + (1 - 2 * c) * step + 16, 8)
            h2 = 1 - h if pair else h
            c2 = 1 - c if other else c
            row = pl.multiple_of(((h2 * 8 + z2) * 2 + c2) * 16, 16)
            rows[pl.ds(row, 16)] = ref[piece * 16 : (piece + 1) * 16]
    out_ref[...] = lax.dot_general(
        basis_ref[...], rows[...], (((1,), (1,)), ((), ())), preferred_element_type=F32
    )


def rotate_grads(place, n0, near, far, basis):
    vmem = pl.BlockSpec(memory_space=pltpu.VMEM)
    return pl.pallas_call(
        rotate_grads_kernel,
        out_shape=jax.ShapeDtypeStruct((256, 512), F32),
        in_specs=[pl.BlockSpec(memory_space=pltpu.SMEM)] + [vmem] * 4,
        out_specs=vmem,
        scratch_shapes=[pltpu.VMEM((512, 1024), BF)],
        compiler_params=pltpu.CompilerParams(vmem_limit_bytes=8 * 1024 * 1024),
        cost_estimate=pl.CostEstimate(flops=2 * 512 * 256 * 1024, bytes_accessed=2 << 20, transcendentals=0),
        name="rotate_grads",
    )(place, n0, near, far, basis)


def arrange_kernel(place_ref, *refs):
    blocks, (mine_ref, theirs_ref, rows) = refs[:8], refs[8:]
    z, c = place_ref[0], place_ref[1]
    for b, ref in enumerate(blocks):
        k = lax.rem((b - z) * (1 - 2 * c) + 16, 8)
        for core in range(2):
            other = jnp.where(c == core, 0, 1)
            centre = jnp.where(k == 0, 224, 192) + other * 256
            ring = jnp.where(k < 4, (k - 1) * 64 + other * 32, 256 + (7 - k) * 64 + (1 - other) * 32)
            row = pl.multiple_of(jnp.where((k == 0) | (k == 4), centre, ring), 32)
            rows[pl.ds(row, 32)] = ref[core * 32 : core * 32 + 32]
    mine_ref[...] = rows[:256]
    theirs_ref[...] = rows[256:]


def arrange(place, blocks):
    vmem = pl.BlockSpec(memory_space=pltpu.VMEM)
    depth = blocks[0].shape[1]
    rows = jax.ShapeDtypeStruct((256, depth), BF)
    return pl.pallas_call(
        arrange_kernel,
        out_shape=(rows, rows),
        in_specs=[pl.BlockSpec(memory_space=pltpu.SMEM)] + [vmem] * 8,
        out_specs=(vmem, vmem),
        scratch_shapes=[pltpu.VMEM((512, depth), BF)],
        compiler_params=pltpu.CompilerParams(vmem_limit_bytes=8 * 1024 * 1024),
        cost_estimate=pl.CostEstimate(flops=0, bytes_accessed=4 * 512 * depth, transcendentals=0),
        name="arrange",
    )(place, *blocks)


def rotate_kernel(cuts, here_rows_ref, away_rows_ref, here_ref, away_ref, *refs):
    out_refs, (here, away, sem) = refs[:STREAMS], refs[STREAMS:]
    copies = []
    for i, (lo, hi) in enumerate(zip(cuts, cuts[1:])):
        rows = pl.ds(lo, hi - lo)
        copies.append(
            [
                pltpu.make_async_copy(ref.at[rows], held.at[rows], sem.at[2 * i + j])
                for j, (ref, held) in enumerate(((here_ref, here), (away_ref, away)))
            ]
        )
    for pair in copies:
        for copy in pair:
            copy.start()
    width = out_refs[0].shape[1]
    for pair, lo, hi in zip(copies, cuts, cuts[1:]):
        for copy in pair:
            copy.wait()
        for t in range(lo, hi, TILE):
            total = dot_t(here_rows_ref[...], here[t : t + TILE]) + dot_t(away_rows_ref[...], away[t : t + TILE])
            out_refs[t // width][:, t % width : t % width + TILE] = total


def rotate(here_rows, away_rows, here, away):
    vmem, hbm = pl.BlockSpec(memory_space=pltpu.VMEM), pl.BlockSpec(memory_space=pl.ANY)
    whole, depth = here.shape
    cuts = list(range(0, whole, 4 * TILE)) + [whole]
    return pl.pallas_call(
        functools.partial(rotate_kernel, cuts),
        out_shape=[jax.ShapeDtypeStruct((256, whole // STREAMS), F32)] * STREAMS,
        in_specs=[vmem, vmem, hbm, hbm],
        out_specs=[vmem] * STREAMS,
        scratch_shapes=[
            pltpu.VMEM((whole, depth), BF),
            pltpu.VMEM((whole, depth), BF),
            pltpu.SemaphoreType.DMA((2 * len(cuts) - 2,)),
        ],
        compiler_params=pltpu.CompilerParams(vmem_limit_bytes=24 * 1024 * 1024),
        cost_estimate=pl.CostEstimate(flops=1024 * depth * whole, bytes_accessed=4 * depth * whole, transcendentals=0),
        name="rotate",
    )(
        here_rows,
        away_rows,
        pltpu.with_memory_space_constraint(here, pltpu.HBM),
        pltpu.with_memory_space_constraint(away, pltpu.HBM),
    )


def shards(activations, out_grads, act_basis, grad_basis):
    mp, dp = lax.axis_index("mp"), lax.axis_index("dp")
    c, z, h = mp % 2, (mp // 2) % 8, mp // 16
    y, l = dp // 2, dp % 2
    place = jnp.stack([z, c, y, l, h]).astype(jnp.int32)

    pair = cat(out_grads, swap(out_grads, "out_grads_pair"))

    def shift(x, b):
        with jax.named_scope(f"activations_{b}"):
            return lax.ppermute(x, "dp", dp_perm(lambda y, l: (y + b // 2, l + b % 2)))

    blocks = [activations] + [None] * 7
    for b in (4, 2, 6, 1):
        blocks[b] = shift(activations, b)
    basis_away = swap(after(act_basis, pair), "basis_away")
    far = across(pair, "far")
    blocks[3] = shift(blocks[1], 2)
    blocks[7] = shift(blocks[1], 6)
    blocks[5] = shift(blocks[4], 1)
    n0 = cat(pair[:16], far[:16], pair[16:], far[16:])
    n2 = ahead2(n0, "n2")
    x_here, theirs = arrange(place, blocks)
    x_away = swap(after(theirs, n2), "x_away")
    n02 = cat(n0, n2)
    n13 = ahead(n02, "n13")
    n4 = ahead2(n2[:32], "n4")

    whole = act_basis.shape[0]
    width = whole // STREAMS
    streams = range(STREAMS)
    p = rotate(x_here, x_away, act_basis, basis_away)

    r = [ahead(p[s][192:224].astype(BF), f"step1_{s}") for s in streams]
    n13, n4 = lax.optimization_barrier((n13, n4, p[0]))[:2]
    near = cat(n2, n13, n4)
    g = rotate_grads(place, n0, near, swap(near, "near_away"), grad_basis)
    g_away = lax.ppermute(g, "dp", Y1)
    r = [cat(p[s][128:160] + r[s].astype(F32), p[s][160:192]).astype(BF) for s in streams]
    r = [ahead(r[s], f"step2_{s}") for s in streams]
    r[0] = after(r[0], g)
    r = [ahead((p[s][64:128] + r[s].astype(F32)).astype(BF), f"step3_{s}") for s in streams]
    r = [ahead((p[s][0:64] + r[s].astype(F32)).astype(BF), f"step4_{s}") for s in streams]
    g = g + g_away
    g_away = lax.ppermute(g, "dp", Y2)
    r[1] = after(r[1], g)
    r = [p[s][224:256] + r[s][:32].astype(F32) + swap(r[s][32:], f"other_{s}").astype(F32) for s in streams]
    own = [(r[s] + across(r[s].astype(BF), f"across_{s}").astype(F32)).astype(BF) for s in streams]

    twin = [swap(own[s], f"twin_{s}") for s in streams]
    a1 = [ahead(cat(own[s], twin[s]), f"a1_{s}") for s in streams]
    g = g + g_away
    g_away = lax.ppermute(g, "dp", XLO)
    a1[0] = after(a1[0], g)
    a2 = [ahead(a1[s], f"a2_{s}") for s in streams]
    b12 = [swap(cat(a1[s], a2[s]), f"b12_{s}") for s in streams]
    a3 = [ahead(a2[s], f"a3_{s}") for s in streams]
    g = (g + g_away).astype(BF)
    a4 = [ahead(after(a3[s][:32], g), f"a4_{s}") for s in streams]
    b34 = [swap(cat(a3[s], a4[s]), f"b34_{s}") for s in streams]
    out = None
    for s in streams:
        parts = [x[s] for x in (own, twin, a1, a2, a3, a4, b12, b34)]
        out = finish(place, g, parts, width, s * width, whole, out)
    return out


def solution(mesh):
    return jax.shard_map(
        shards,
        mesh=mesh,
        in_specs=(P("dp", "mp"), P("mp", "dp"), P("dp", "mp"), P("mp", "dp")),
        out_specs=P("mp", "dp"),
        check_vma=False,
    )
```

```python
import functools

import jax
import jax.numpy as jnp
from jax import lax
from jax.experimental import pallas as pl
from jax.experimental.pallas import tpu as pltpu
from jax.sharding import PartitionSpec as P

SEQ_LEN = 256
BF, F32 = jnp.bfloat16, jnp.float32
TILE = 256
STREAMS = 2


def mp_at(h, z, c):
    return ((h % 2) * 8 + z % 8) * 2 + c % 2


def dp_at(y, l):
    return (y % 4) * 2 + l % 2


def mp_perm(f):
    return [(mp_at(h, z, c), mp_at(*f(h, z, c))) for h in range(2) for z in range(8) for c in range(2)]


def dp_perm(f):
    return [(dp_at(y, l), dp_at(*f(y, l))) for y in range(4) for l in range(2)]


CORE = mp_perm(lambda h, z, c: (h, z, c + 1))
XHI = mp_perm(lambda h, z, c: (h + 1, z, c))
AHEAD = mp_perm(lambda h, z, c: (h, z + 1 - 2 * c, c))
AHEAD2 = mp_perm(lambda h, z, c: (h, z + 2 - 4 * c, c))
XLO = dp_perm(lambda y, l: (y, l + 1))
Y1 = dp_perm(lambda y, l: (y ^ 1, l))
Y2 = dp_perm(lambda y, l: (y ^ 2, l))


def swap(x, name="swap"):
    with jax.named_scope(name):
        return lax.ppermute(x, "mp", CORE)


def ahead(x, name="ahead"):
    with jax.named_scope(name):
        return lax.ppermute(x, "mp", AHEAD)


def ahead2(x, name="ahead2"):
    with jax.named_scope(name):
        return lax.ppermute(x, "mp", AHEAD2)


def across(x, name="across"):
    with jax.named_scope(name):
        return lax.ppermute(x, "mp", XHI)


def after(x, *others):
    return lax.optimization_barrier((x,) + others)[0]


def dot_t(a, b):
    return lax.dot_general(a, b, (((1,), (1,)), ((), ())), preferred_element_type=F32)


def cat(*parts):
    return jnp.concatenate(parts)


def block(step):
    return [(step, 0), (step, 1)]


def mirrored(halves):
    return [(-step if abs(step) < 4 else step, 1 - other) for step, other in halves]


LAYOUT = [[(0, 0)], [(0, 1)], block(-1), block(-2), block(-3), [(4, 0)]]
LAYOUT = LAYOUT + [mirrored(block(-1) + block(-2) + block(-3) + [(4, 0)])]


def finish_kernel(width, first, aliased, place_ref, g_ref, *refs):
    blocks, refs = refs[: len(LAYOUT)], refs[len(LAYOUT) + aliased :]
    out_ref, act, tile, out_sem = refs
    z, c, y, l = [place_ref[i] for i in range(4)]
    for ref, halves in zip(blocks, LAYOUT):
        for i, (step, other) in enumerate(halves):
            b = lax.rem(z + (1 - 2 * c) * step + 16, 8)
            source = lax.rem(y + 4 - b // 2, 4) * 2 + lax.rem(l + b, 2)
            row = pl.multiple_of(source * 64 + (1 - c if other else c) * 32, 32)
            act[pl.ds(row, 32)] = ref[i * 32 : (i + 1) * 32]
    writes = []
    for t in range(width // TILE):
        total = None
        for s in range(2):
            rows = slice(s * SEQ_LEN, (s + 1) * SEQ_LEN)
            part = jnp.dot(g_ref[:, rows], act[rows, t * TILE : (t + 1) * TILE], preferred_element_type=F32)
            total = part * part if total is None else total + part * part
        tile[t] = total * F32(1 / 512)
        write = pltpu.make_async_copy(tile.at[t], out_ref.at[:, pl.ds(first + t * TILE, TILE)], out_sem.at[t])
        write.start()
        writes.append(write)
    for write in writes:
        write.wait()


def finish(place, g, blocks, width, first, whole, rest):
    aliased = rest is not None
    vmem, hbm = pl.BlockSpec(memory_space=pltpu.VMEM), pl.BlockSpec(memory_space=pl.ANY)
    tiles = width // TILE
    return pl.pallas_call(
        functools.partial(finish_kernel, width, first, int(aliased)),
        out_shape=jax.ShapeDtypeStruct((256, whole), F32),
        in_specs=[pl.BlockSpec(memory_space=pltpu.SMEM)] + [vmem] * (1 + len(blocks)) + [hbm] * aliased,
        out_specs=hbm,
        scratch_shapes=[
            pltpu.VMEM((512, width), BF),
            pltpu.VMEM((tiles, 256, TILE), F32),
            pltpu.SemaphoreType.DMA((tiles,)),
        ],
        input_output_aliases={2 + len(blocks): 0} if aliased else {},
        compiler_params=pltpu.CompilerParams(vmem_limit_bytes=12 * 1024 * 1024),
        cost_estimate=pl.CostEstimate(flops=2 * 512 * 256 * width, bytes_accessed=width * (1024 + 1024), transcendentals=0),
        name="finish",
    )(place, g, *blocks, *([rest] if aliased else []))


def quarters(halves):
    return [(step, other, pair) for step, other in halves for pair in (0, 1)]


N0 = quarters(block(0))
NEAR = quarters(block(-2) + block(-1) + block(-3) + [(4, 0)])
FAR = quarters(mirrored(block(-2) + block(-1) + block(-3) + [(4, 0)]))


def rotate_grads_kernel(place_ref, n0_ref, near_ref, far_ref, basis_ref, out_ref, rows):
    z, c, h = place_ref[0], place_ref[1], place_ref[4]
    for ref, pieces in ((n0_ref, N0), (near_ref, NEAR), (far_ref, FAR)):
        for piece, (step, other, pair) in enumerate(pieces):
            z2 = lax.rem(z + (1 - 2 * c) * step + 16, 8)
            h2 = 1 - h if pair else h
            c2 = 1 - c if other else c
            row = pl.multiple_of(((h2 * 8 + z2) * 2 + c2) * 16, 16)
            rows[pl.ds(row, 16)] = ref[piece * 16 : (piece + 1) * 16]
    out_ref[...] = lax.dot_general(
        basis_ref[...], rows[...], (((1,), (1,)), ((), ())), preferred_element_type=F32
    )


def rotate_grads(place, n0, near, far, basis):
    vmem = pl.BlockSpec(memory_space=pltpu.VMEM)
    return pl.pallas_call(
        rotate_grads_kernel,
        out_shape=jax.ShapeDtypeStruct((256, 512), F32),
        in_specs=[pl.BlockSpec(memory_space=pltpu.SMEM)] + [vmem] * 4,
        out_specs=vmem,
        scratch_shapes=[pltpu.VMEM((512, 1024), BF)],
        compiler_params=pltpu.CompilerParams(vmem_limit_bytes=8 * 1024 * 1024),
        cost_estimate=pl.CostEstimate(flops=2 * 512 * 256 * 1024, bytes_accessed=2 << 20, transcendentals=0),
        name="rotate_grads",
    )(place, n0, near, far, basis)


def arrange_kernel(place_ref, *refs):
    blocks, (mine_ref, theirs_ref, rows) = refs[:8], refs[8:]
    z, c = place_ref[0], place_ref[1]
    for b, ref in enumerate(blocks):
        k = lax.rem((b - z) * (1 - 2 * c) + 16, 8)
        for core in range(2):
            other = jnp.where(c == core, 0, 1)
            centre = jnp.where(k == 0, 224, 192) + other * 256
            ring = jnp.where(k < 4, (k - 1) * 64 + other * 32, 256 + (7 - k) * 64 + (1 - other) * 32)
            row = pl.multiple_of(jnp.where((k == 0) | (k == 4), centre, ring), 32)
            rows[pl.ds(row, 32)] = ref[core * 32 : core * 32 + 32]
    mine_ref[...] = rows[:256]
    theirs_ref[...] = rows[256:]


def arrange(place, blocks):
    vmem = pl.BlockSpec(memory_space=pltpu.VMEM)
    depth = blocks[0].shape[1]
    rows = jax.ShapeDtypeStruct((256, depth), BF)
    return pl.pallas_call(
        arrange_kernel,
        out_shape=(rows, rows),
        in_specs=[pl.BlockSpec(memory_space=pltpu.SMEM)] + [vmem] * 8,
        out_specs=(vmem, vmem),
        scratch_shapes=[pltpu.VMEM((512, depth), BF)],
        compiler_params=pltpu.CompilerParams(vmem_limit_bytes=8 * 1024 * 1024),
        cost_estimate=pl.CostEstimate(flops=0, bytes_accessed=4 * 512 * depth, transcendentals=0),
        name="arrange",
    )(place, *blocks)


def rotate_kernel(cuts, here_rows_ref, away_rows_ref, here_ref, away_ref, *refs):
    out_refs, (here, away, sem) = refs[:STREAMS], refs[STREAMS:]
    copies = []
    for i, (lo, hi) in enumerate(zip(cuts, cuts[1:])):
        rows = pl.ds(lo, hi - lo)
        copies.append(
            [
                pltpu.make_async_copy(ref.at[rows], held.at[rows], sem.at[2 * i + j])
                for j, (ref, held) in enumerate(((here_ref, here), (away_ref, away)))
            ]
        )
    for pair in copies:
        for copy in pair:
            copy.start()
    width = out_refs[0].shape[1]
    for pair, lo, hi in zip(copies, cuts, cuts[1:]):
        for copy in pair:
            copy.wait()
        for t in range(lo, hi, TILE):
            total = dot_t(here_rows_ref[...], here[t : t + TILE]) + dot_t(away_rows_ref[...], away[t : t + TILE])
            out_refs[t // width][:, t % width : t % width + TILE] = total


def rotate(here_rows, away_rows, here, away):
    vmem, hbm = pl.BlockSpec(memory_space=pltpu.VMEM), pl.BlockSpec(memory_space=pl.ANY)
    whole, depth = here.shape
    cuts = list(range(0, whole, 4 * TILE)) + [whole]
    return pl.pallas_call(
        functools.partial(rotate_kernel, cuts),
        out_shape=[jax.ShapeDtypeStruct((256, whole // STREAMS), F32)] * STREAMS,
        in_specs=[vmem, vmem, hbm, hbm],
        out_specs=[vmem] * STREAMS,
        scratch_shapes=[
            pltpu.VMEM((whole, depth), BF),
            pltpu.VMEM((whole, depth), BF),
            pltpu.SemaphoreType.DMA((2 * len(cuts) - 2,)),
        ],
        compiler_params=pltpu.CompilerParams(vmem_limit_bytes=24 * 1024 * 1024),
        cost_estimate=pl.CostEstimate(flops=1024 * depth * whole, bytes_accessed=4 * depth * whole, transcendentals=0),
        name="rotate",
    )(
        here_rows,
        away_rows,
        pltpu.with_memory_space_constraint(here, pltpu.HBM),
        pltpu.with_memory_space_constraint(away, pltpu.HBM),
    )


def shards(activations, out_grads, act_basis, grad_basis):
    mp, dp = lax.axis_index("mp"), lax.axis_index("dp")
    c, z, h = mp % 2, (mp // 2) % 8, mp // 16
    y, l = dp // 2, dp % 2
    place = jnp.stack([z, c, y, l, h]).astype(jnp.int32)

    pair = cat(out_grads, swap(out_grads, "out_grads_pair"))

    def shift(x, b):
        with jax.named_scope(f"activations_{b}"):
            return lax.ppermute(x, "dp", dp_perm(lambda y, l: (y + b // 2, l + b % 2)))

    blocks = [activations] + [None] * 7
    for b in (4, 2, 6, 1):
        blocks[b] = shift(activations, b)
    basis_away = swap(after(act_basis, pair), "basis_away")
    far = across(pair, "far")
    blocks[3] = shift(blocks[1], 2)
    blocks[7] = shift(blocks[1], 6)
    blocks[5] = shift(blocks[4], 1)
    n0 = cat(pair[:16], far[:16], pair[16:], far[16:])
    n2 = ahead2(n0, "n2")
    x_here, theirs = arrange(place, blocks)
    x_away = swap(after(theirs, n2), "x_away")
    n02 = cat(n0, n2)
    n13 = ahead(n02, "n13")
    n4 = ahead2(n2[:32], "n4")

    whole = act_basis.shape[0]
    width = whole // STREAMS
    streams = range(STREAMS)
    p = rotate(x_here, x_away, act_basis, basis_away)

    r = [ahead(p[s][192:224].astype(BF), f"step1_{s}") for s in streams]
    n13, n4 = lax.optimization_barrier((n13, n4, p[0]))[:2]
    near = cat(n2, n13, n4)
    g = rotate_grads(place, n0, near, swap(near, "near_away"), grad_basis)
    g_away = lax.ppermute(g, "dp", Y1)
    r = [cat(p[s][128:160] + r[s].astype(F32), p[s][160:192]).astype(BF) for s in streams]
    r = [ahead(r[s], f"step2_{s}") for s in streams]
    r[0] = after(r[0], g)
    r = [ahead((p[s][64:128] + r[s].astype(F32)).astype(BF), f"step3_{s}") for s in streams]
    r = [ahead((p[s][0:64] + r[s].astype(F32)).astype(BF), f"step4_{s}") for s in streams]
    g = g + g_away
    g_away = lax.ppermute(g, "dp", Y2)
    r[1] = after(r[1], g)
    r = [p[s][224:256] + r[s][:32].astype(F32) + swap(r[s][32:], f"other_{s}").astype(F32) for s in streams]
    own = [(r[s] + across(r[s].astype(BF), f"across_{s}").astype(F32)).astype(BF) for s in streams]

    twin = [swap(own[s], f"twin_{s}") for s in streams]
    a1 = [ahead(cat(own[s], twin[s]), f"a1_{s}") for s in streams]
    g = g + g_away
    g_away = lax.ppermute(g, "dp", XLO)
    a1[0] = after(a1[0], g)
    a2 = [ahead(a1[s], f"a2_{s}") for s in streams]
    a3 = [ahead(a2[s], f"a3_{s}") for s in streams]
    g = (g + g_away).astype(BF)
    a4 = [ahead(after(a3[s][:32], g), f"a4_{s}") for s in streams]
    others = [swap(cat(a1[s], a2[s], a3[s], a4[s]), f"others_{s}") for s in streams]
    out = None
    for s in streams:
        parts = [x[s] for x in (own, twin, a1, a2, a3, a4, others)]
        out = finish(place, g, parts, width, s * width, whole, out)
    return out


def solution(mesh):
    return jax.shard_map(
        shards,
        mesh=mesh,
        in_specs=(P("dp", "mp"), P("mp", "dp"), P("dp", "mp"), P("mp", "dp")),
        out_specs=P("mp", "dp"),
        check_vma=False,
    )
```
